128 devices in a mesh: visit: 4 (over y), ccd: 32 (over x, z, core).
Axes of the slice: x: 4, y: 4, z: 4, core: 2. Of those that a mesh axis runs over, the one named last changes fastest.
Arguments:
- exposure: bfloat16 [4, 2048, 4096], P('visit', 'ccd'), may hold values from -6 to 6
- offsets: int32 [4, 32, 2], P('visit', 'ccd'), may hold values from -32 to 32
- fraction: float32 [4, 32, 2], P('visit', 'ccd'), may hold values from 0 to 1
- route_patch: int32 [4, 2048], P('visit', 'ccd'), may hold values from 0 to 127, as said below
- route_slot: int32 [4, 2048], P('visit', 'ccd'), may hold values from 0 to 63
- block_weight: bfloat16 [4, 2048], P('visit', 'ccd'), may hold values from 0.25 to 4
- kernel_rows: float32 [33], replicated, may hold values from -1 to 1
- kernel_columns: float32 [33], replicated, may hold values from -1 to 1
Outputs:
- coadded: bfloat16 [512, 65536], P('visit', 'ccd')
- matched: float32 [512, 65536], P('visit', 'ccd')
The draws below stay inside these ranges and needn't reach their ends.
Inputs may be any that keep to these rules, and one draw needn't show every extreme that they name: `route_patch`: no patch is named by more than 2 of one exposure's 64 blocks; one patch, drawn from the seed, is named by exactly 2 blocks of every exposure.
All inputs are finite; a program needn't handle non-finite values.
Results may differ from the reference program's by a relative error of at most 0.0082.
Values may be sent and summed in bfloat16 or wider, within the bound.
A program may use at most 64 MiB of HBM per device.

```python
import math
import jax
import jax.numpy as jnp
from jax import lax

COLS = 4096
ROWS_DEV = 64
BLOCK_ROWS = 32
BLOCK_COLS = 128
MAX_OFFSET = 32
MARGIN = 40
HALF_KERNEL = 16
VISITS = 4
CCDS = 32
PATCHES = 128
FOCAL_ROWS = 2048
BLOCKS = 64
CAP = 2
SLOTS = 64
PATCH_ROWS = 128
PATCH_COLS = 2048
SLOT_ROWS = 4
SLOT_COLS = 16
TAPS = 33


def draw_route_patch(key, part):
    deep_key, rest_key = jax.random.split(jax.random.fold_in(key, 11))
    deepest = jax.random.randint(deep_key, (), 0, PATCHES)

    def one_source(source_key):
        count_key, order_key, place_key = jax.random.split(source_key, 3)
        others = jax.random.permutation(order_key, PATCHES - 1).astype(jnp.int32)
        others = others + (others >= deepest).astype(jnp.int32)
        counts = jax.random.randint(count_key, (PATCHES - 1,), CAP // 2, CAP + 1)
        ends = jnp.cumsum(counts)
        position = jnp.arange(BLOCKS - CAP, dtype=jnp.int32)
        which = jnp.sum((position[:, None] >= ends[None, :]).astype(jnp.int32), axis=1)
        listed = jnp.concatenate([jnp.full((CAP,), deepest, jnp.int32), others[which].astype(jnp.int32)])
        shuffle = jax.random.permutation(place_key, BLOCKS)
        return listed[shuffle]
    source_keys = jax.random.split(rest_key, PATCHES)
    routes = jax.vmap(one_source)(source_keys)
    return routes.reshape(VISITS, CCDS * BLOCKS).astype(jnp.int32)


def set_ends(result, rng, least, largest):
    longest = result.shape.index(max(result.shape))
    spots = []
    for shift in (0, 1):
        where = [jax.random.randint(jax.random.fold_in(rng, axis), (), 0, length) for axis, length in enumerate(result.shape)]
        where[longest] = (where[longest] + shift) % result.shape[longest]
        spots.append(tuple(where))
    return result.at[spots[0]].set(least).at[spots[1]].set(largest)


def block_levels(rng, shape, pieces, smallest, high):
    level = 1.0
    for dim, parts in pieces:
        steps = jax.random.uniform(jax.random.fold_in(jax.random.fold_in(rng, 6), dim), (parts,), jnp.float32, smallest / len(pieces), high / len(pieces))
        level = level * jnp.repeat(jnp.exp(steps), shape[dim] // parts).reshape((-1,) + (1,) * (len(shape) - 1 - dim))
    return level


def bell_draw(rng, shape, deviation, limit, cuts=(), held_as=jnp.bfloat16):
    gain = block_levels(rng, shape, cuts, -0.22, 0.18) if cuts else 1.0
    values = jax.random.normal(rng, shape, jnp.float32) * deviation * gain
    return jnp.minimum(jnp.maximum(values, -limit), limit).astype(held_as)


def setup_inputs(seed: int = 0) -> dict:
    keys = jax.random.split(jax.random.key(seed), 9)
    exposure = bell_draw(keys[0], (VISITS, FOCAL_ROWS, COLS), 1.0, 6.0, ((0, 4), (1, 32)))
    offsets = set_ends(jax.random.randint(keys[1], (VISITS, CCDS, 2), 0 - MAX_OFFSET, MAX_OFFSET + 1), jax.random.fold_in(keys[1], 1), 0 - MAX_OFFSET, MAX_OFFSET).astype(jnp.int32)
    fraction = jnp.clip(1.0 * jax.random.uniform(keys[2], (VISITS, CCDS, 2), jnp.float32) ** block_levels(keys[2], (VISITS, CCDS, 2), ((0, 4), (1, 32)), -0.2, 0.2), 0.0, 1.0)
    route_patch = draw_route_patch(jax.random.fold_in(keys[8], 71), 0)
    route_slot = set_ends(jax.random.randint(keys[4], (VISITS, CCDS * BLOCKS), 0, SLOTS), jax.random.fold_in(keys[4], 1), 0, SLOTS - 1).astype(jnp.int32)
    block_weight = jnp.clip(jnp.exp(math.log(4.0) - 2.7725887 * jax.random.uniform(keys[5], (VISITS, CCDS * BLOCKS), jnp.float32) ** block_levels(keys[5], (VISITS, CCDS * BLOCKS), ((0, 4), (1, 32)), -0.2, 0.2)), 0.25, 4.0).astype(jnp.bfloat16)
    kernel_rows = bell_draw(keys[6], (TAPS,), TAPS ** -0.5, 1.0, (), jnp.float32)
    kernel_columns = bell_draw(keys[7], (TAPS,), TAPS ** -0.5, 1.0, (), jnp.float32)
    return {"exposure": exposure, "offsets": offsets, "fraction": fraction, "route_patch": route_patch, "route_slot": route_slot, "block_weight": block_weight, "kernel_rows": kernel_rows, "kernel_columns": kernel_columns}


def lanczos_weights(fraction_part):
    distance = jnp.arange(3, -3, -1).astype(jnp.float32) - fraction_part
    kernel = jnp.sinc(distance) * jnp.sinc(distance / 3.0)
    return (kernel / jnp.sum(kernel)).astype(jnp.bfloat16)


def reference(exposure, offsets, fraction, route_patch, route_slot, block_weight, kernel_rows, kernel_columns):
    padded = jnp.pad(exposure, ((0, 0), (MARGIN, MARGIN), (0, 0)))

    def warp_one(source):
        visit_index = source // CCDS
        ccd_index = source % CCDS
        shift_rows = offsets[visit_index, ccd_index, 0].astype(jnp.int32)
        shift_columns = offsets[visit_index, ccd_index, 1].astype(jnp.int32)
        row_weights = lax.optimization_barrier(lanczos_weights(fraction[visit_index, ccd_index, 0])).astype(jnp.float32)
        column_weights = lax.optimization_barrier(lanczos_weights(fraction[visit_index, ccd_index, 1])).astype(jnp.float32)
        focal = lax.dynamic_index_in_dim(padded, visit_index, 0, keepdims=False)
        summed = jnp.zeros((ROWS_DEV, COLS), jnp.float32)
        for tap_index in range(6):
            first_row = (ccd_index * ROWS_DEV + MARGIN - shift_rows - (3 - tap_index)).astype(jnp.int32)
            summed = summed + row_weights[tap_index] * lax.dynamic_slice_in_dim(focal, first_row, ROWS_DEV, 0).astype(jnp.float32)
        row_warped = summed.astype(jnp.bfloat16)
        widened = jnp.pad(row_warped, ((0, 0), (128, 128)))
        summed = jnp.zeros((ROWS_DEV, COLS), jnp.float32)
        for tap_index in range(6):
            first_column = (128 - shift_columns - (3 - tap_index)).astype(jnp.int32)
            summed = summed + column_weights[tap_index] * lax.dynamic_slice_in_dim(widened, first_column, COLS, 1).astype(jnp.float32)
        return summed.astype(jnp.bfloat16)

    warped = lax.map(warp_one, jnp.arange(PATCHES, dtype=jnp.int32))
    blocks = warped.reshape(PATCHES, ROWS_DEV // BLOCK_ROWS, BLOCK_ROWS, COLS // BLOCK_COLS, BLOCK_COLS)
    blocks = blocks.transpose(0, 1, 3, 2, 4).reshape(PATCHES * BLOCKS, BLOCK_ROWS * BLOCK_COLS)
    destination = (route_patch.reshape(-1) * SLOTS + route_slot.reshape(-1)).astype(jnp.int32)
    weights = block_weight.reshape(-1).astype(jnp.float32)
    numerator = jax.ops.segment_sum(blocks.astype(jnp.float32) * weights[:, None], destination, num_segments=PATCHES * SLOTS)
    weight_total = jax.ops.segment_sum(weights, destination, num_segments=PATCHES * SLOTS)
    slot_values = (numerator / jnp.maximum(weight_total, 1.0)[:, None]).astype(jnp.bfloat16)
    coadded = slot_values.reshape(VISITS, CCDS, SLOT_ROWS, SLOT_COLS, BLOCK_ROWS, BLOCK_COLS)
    coadded = coadded.transpose(0, 2, 4, 1, 3, 5).reshape(VISITS * PATCH_ROWS, CCDS * PATCH_COLS)
    row_kernel = lax.optimization_barrier(kernel_rows.astype(jnp.bfloat16)).astype(jnp.float32)
    column_kernel = lax.optimization_barrier(kernel_columns.astype(jnp.bfloat16)).astype(jnp.float32)
    framed = jnp.pad(coadded, HALF_KERNEL)
    tract_rows = VISITS * PATCH_ROWS
    tract_columns = CCDS * PATCH_COLS
    summed = jnp.zeros((tract_rows, tract_columns + 2 * HALF_KERNEL), jnp.float32)
    for tap_index in range(TAPS):
        summed = summed + row_kernel[tap_index] * framed[tap_index:tap_index + tract_rows].astype(jnp.float32)
    smoothed = summed.astype(jnp.bfloat16)
    matched = jnp.zeros((tract_rows, tract_columns), jnp.float32)
    for tap_index in range(TAPS):
        matched = matched + column_kernel[tap_index] * smoothed[:, tap_index:tap_index + tract_columns].astype(jnp.float32)
    return coadded, matched
```

```python
import functools
import math

import jax
import jax.numpy as jnp
from jax import lax
from jax.experimental import pallas as pl
from jax.experimental.pallas import tpu as pltpu
from jax.sharding import PartitionSpec as P

MESH = pl.DeviceIdType.MESH
N = 128
ROWS = 64
COLS = 4096
EDGE = 48
EXT = ROWS + 2 * EDGE
TILES = COLS // 128
TAPS = 33
RIM = 16
PROWS, PCOLS = 128, 2048
F32, BF16, I32 = jnp.float32, jnp.bfloat16, jnp.int32


def iota(shape, dim):
    return lax.broadcasted_iota(I32, shape, dim)


def dot(a, b):
    return jnp.dot(a, b, preferred_element_type=F32)


def sinc(t):
    x = math.pi * t
    zero = t == 0.0
    x = jnp.where(zero, 1.0, x)
    return jnp.where(zero, 1.0, jnp.sin(x) / x)


def lanczos(f):
    k = iota((8, 128), 0)
    t = (3 - k).astype(F32) - f
    w = jnp.where(k < 6, sinc(t) * sinc(t / 3.0), 0.0)
    return w / jnp.sum(w, axis=0, keepdims=True)


def band(lag, weights):
    m = jnp.zeros(lag.shape, F32)
    for k, w in enumerate(weights):
        m = jnp.where(lag == k, w, m)
    return m


def kernel(
    exposure, offsets, fraction, idx_s, route_patch, route_slot, block_weight, kernel_rows, kernel_columns,
    coadded, matched,
    ext, rwb, wb, sbuf, rbuf, gf, nf, fr, sb, row_m, col_m, frow_m, fcol_m, a_m, meta,
    sem_in, sem_mg, sem_meta_s, sem_meta_r, sem_s, sem_r, sem_rim,
):
    v = lax.axis_index("visit")
    c = lax.axis_index("ccd")
    me = v * 32 + c
    core = lax.rem(c, 2)
    z = lax.rem(c // 2, 4)
    x = c // 8

    def peer(dv, dx, dz, dc):
        return (
            lax.rem(v + dv, 4),
            (lax.rem(x + dx, 4) * 4 + lax.rem(z + dz, 4)) * 2 + lax.rem(core + dc, 2),
        )

    def remote(src, dst, s, r, to):
        return pltpu.make_async_remote_copy(
            src_ref=src, dst_ref=dst, send_sem=s, recv_sem=r, device_id=to, device_id_type=MESH
        )

    c_next, c_prev = lax.rem(c + 1, 32), lax.rem(c + 31, 32)
    v_next, v_prev = lax.rem(v + 1, 4), lax.rem(v + 3, 4)

    bar = pltpu.get_barrier_semaphore()
    first = [peer(0, 0, 0, 1), (v, c_next), (v, c_prev)]
    for i in (1, 2, 3):
        first += [peer(i, 0, 0, 0), peer(0, i, 0, 0), peer(0, 0, i, 0)]
    for to in first:
        pl.semaphore_signal(bar, inc=1, device_id=to, device_id_type=MESH)

    own = pltpu.make_async_copy(exposure.at[0], ext.at[pl.ds(EDGE, ROWS)], sem_in)
    own.start()

    code = (route_patch[...] * 64 + route_slot[...]).astype(F32)
    meta[me] = jnp.concatenate([code, block_weight[...].astype(F32)], axis=1)

    pl.semaphore_wait(bar, len(first))

    margins = [
        remote(exposure.at[0, pl.ds(ROWS - EDGE, EDGE)], ext.at[pl.ds(0, EDGE)], sem_mg.at[0], sem_mg.at[1], (v, c_next)),
        remote(exposure.at[0, pl.ds(0, EDGE)], ext.at[pl.ds(EDGE + ROWS, EDGE)], sem_mg.at[2], sem_mg.at[3], (v, c_prev)),
    ]
    for copy in margins:
        copy.start()

    def stage(number, start, rows, peers):
        copies = []
        for i, to in enumerate(peers):
            piece = meta.at[pl.ds(start, rows)]
            copies.append(remote(piece, piece, sem_meta_s.at[number, i], sem_meta_r.at[number, i], to))
        for copy in copies:
            copy.start()
        return copies

    def finish(copies):
        for copy in copies:
            copy.wait()

    going = stage(0, me, 1, [peer(0, 0, 0, 1)])
    w_row = lanczos(fraction[0, 0, 0]).astype(BF16).astype(F32)
    lag = iota((ROWS, EXT), 1) - iota((ROWS, EXT), 0) - (EDGE - 3 - offsets[0, 0, 0])
    m = band(lag, [w_row[k : k + 1, 0:1] for k in range(6)])
    at = iota((ROWS, EXT), 1)
    outside = ((at < EDGE) & (c == 0)) | ((at >= EDGE + ROWS) & (c == 31))
    row_m[...] = jnp.where(outside, 0.0, m).astype(BF16)
    finish(going)

    going = stage(1, me - core, 2, [peer(0, 0, i, 0) for i in (1, 2, 3)])
    w_col = lanczos(fraction[0, 0, 1]).astype(BF16).astype(F32)
    lag = iota((384, 128), 0) - iota((384, 128), 1) - (125 - offsets[0, 0, 1])
    col_m[...] = band(lag, [w_col[k : k + 1, 0:1] for k in range(6)]).astype(BF16)
    finish(going)

    going = stage(2, v * 32 + x * 8, 8, [peer(0, i, 0, 0) for i in (1, 2, 3)])
    blank = jnp.zeros((64, 128), BF16)
    rwb[pl.ds(0, 64), :] = blank
    rwb[pl.ds(33 * 64, 64), :] = blank
    own.wait()
    finish(going)

    going = stage(3, v * 32, 32, [peer(i, 0, 0, 0) for i in (1, 2, 3)])
    for copy in margins:
        copy.wait()

    def row_pass(i, _):
        got = dot(row_m[...], ext[:, pl.ds(pl.multiple_of(i * 256, 256), 256)]).astype(BF16)
        at = pl.multiple_of(i * 128, 128)
        rwb[pl.ds(at + 64, 64), :] = got[:, :128]
        rwb[pl.ds(at + 128, 64), :] = got[:, 128:]
        return 0

    lax.fori_loop(0, TILES // 2, row_pass, 0, unroll=4)

    def column_pass(i, _):
        at = pl.multiple_of(i * 256, 256)
        three = jnp.concatenate([rwb[pl.ds(at + 64 * p, 256), :] for p in range(3)], axis=1)
        wb[pl.ds(i * 8, 8)] = dot(three, col_m[...]).astype(BF16).reshape(8, 32, 128)
        return 0

    lax.fori_loop(0, TILES // 4, column_pass, 0, unroll=2)
    finish(going)

    def pick(p, out, o):
        for k in range(2):
            out[o, pl.ds(32 * k, 32), :] = wb[idx_s[N * k + p]]

    def send(d, _):
        e = lax.rem(d * 37, N)
        pv, pc = peer(e // 32, lax.rem(e // 8, 4), lax.rem(e // 2, 4), lax.rem(e, 2))
        p = pv * 32 + pc
        pick(p, sbuf, d)
        remote(sbuf.at[d], rbuf.at[me], sem_s, sem_r, (pv, pc)).start()
        return 0

    lax.fori_loop(1, N, send, 0)
    pick(me, rbuf, me)

    lag = iota((PROWS, PROWS + 2 * RIM), 1) - iota((PROWS, PROWS + 2 * RIM), 0)
    m = band(lag, [kernel_rows[k] for k in range(TAPS)])
    at = iota((PROWS, PROWS + 2 * RIM), 1)
    outside = ((at < RIM) & (v == 0)) | ((at >= RIM + PROWS) & (v == 3))
    frow_m[...] = jnp.where(outside, 0.0, m).astype(BF16)
    lag = iota((384, 128), 0) - iota((384, 128), 1) - (128 - RIM)
    fcol_m[...] = band(lag, [kernel_columns[k] for k in range(TAPS)]).astype(BF16)

    every = meta[:, 0, :]
    weight = pltpu.roll(every, 64, 1)
    patch = jnp.floor(every * (1.0 / 64.0))
    slot = every - patch * 64.0
    lane = iota((N, N), 1)
    match = (patch == me.astype(F32)) & (lane < 64)
    earlier = jnp.where(iota((N, N), 0) < iota((N, N), 1), 1.0, 0.0).astype(BF16)
    rank = dot(jnp.where(match, 1.0, 0.0).astype(BF16), earlier)
    total = jnp.zeros((64, 1), F32)
    for k in range(2):
        chosen = match & (rank == float(k))
        s_k = jnp.sum(jnp.where(chosen, slot, 0.0), axis=1, keepdims=True)
        w_k = jnp.sum(jnp.where(chosen, weight, 0.0), axis=1, keepdims=True)
        table = jnp.where(lane.astype(F32) == s_k, w_k, 0.0).T[:64]
        total = total + jnp.sum(table, axis=1, keepdims=True)
        a_m[:, pl.ds(128 * k, 128)] = table.astype(BF16)
    scale = 1.0 / jnp.maximum(total, 1.0)

    pltpu.make_async_copy(sbuf.at[pl.ds(1, N - 1)], sbuf.at[pl.ds(1, N - 1)], sem_s).wait()
    pltpu.make_async_copy(rbuf.at[pl.ds(1, N - 1)], rbuf.at[pl.ds(1, N - 1)], sem_r).wait()

    def widen(s, _):
        gf[pl.ds(pl.multiple_of(s * 64, 64), 64), :] = rbuf[s].astype(F32)
        return 0

    lax.fori_loop(0, N, widen, 0, unroll=8)

    def coadd(i, _):
        pair = []
        for y in (2 * i, 2 * i + 1):
            halves = [gf[pl.ds(32 * k + y, N, stride=64), :] for k in range(2)]
            pair.append(jnp.concatenate(halves, axis=0).astype(BF16))
        got = dot(a_m[...], jnp.concatenate(pair, axis=1)) * scale
        nf[pl.ds(pl.multiple_of(i * 128, 128), 64), :] = got[:, :128]
        nf[pl.ds(pl.multiple_of(i * 128 + 64, 64), 64), :] = got[:, 128:]
        return 0

    lax.fori_loop(0, 16, coadd, 0, unroll=4)

    def lay(j, _):
        at = pl.multiple_of(j * 128, 128)
        for i in range(4):
            tile = nf[pl.ds(i * 16 + j, 32, stride=64), :].astype(BF16)
            fr[pl.ds(RIM + 32 * i, 32), pl.ds(at + 128, 128)] = tile
            coadded[pl.ds(32 * i, 32), pl.ds(at, 128)] = tile
        return 0

    lax.fori_loop(0, 16, lay, 0, unroll=4)

    top, bottom, centre = pl.ds(RIM, RIM), pl.ds(PROWS, RIM), pl.ds(RIM, PROWS)
    above, below = pl.ds(0, RIM), pl.ds(RIM + PROWS, RIM)
    west, east, across = pl.ds(128, 128), pl.ds(PCOLS, 128), pl.ds(128, PCOLS)
    left, right = pl.ds(0, 128), pl.ds(128 + PCOLS, 128)
    rims = []
    for n, (rows, cols, to_rows, to_cols, to) in enumerate(
        (
            (bottom, across, above, across, (v_next, c)),
            (top, across, below, across, (v_prev, c)),
            (centre, east, centre, left, (v, c_next)),
            (centre, west, centre, right, (v, c_prev)),
            (bottom, east, above, left, (v_next, c_next)),
            (bottom, west, above, right, (v_next, c_prev)),
            (top, east, below, left, (v_prev, c_next)),
            (top, west, below, right, (v_prev, c_prev)),
        )
    ):
        copy = remote(fr.at[rows, cols], fr.at[to_rows, to_cols], sem_rim.at[0, n], sem_rim.at[1, n], to)
        copy.start()
        rims.append(copy)
    for copy in rims:
        copy.wait()

    def smooth(i, _):
        got = dot(frow_m[...], fr[:, pl.ds(pl.multiple_of(i * 256, 256), 256)]).astype(BF16)
        at = pl.multiple_of(i * 256, 256)
        sb[pl.ds(at, 128), :] = got[:, :128]
        sb[pl.ds(at + 128, 128), :] = got[:, 128:]
        return 0

    lax.fori_loop(0, 9, smooth, 0, unroll=3)
    blank = jnp.zeros((128, 128), BF16)
    sb[pl.ds(0, 128), :] = jnp.where(c == 0, blank, sb[pl.ds(0, 128), :])
    sb[pl.ds(17 * 128, 128), :] = jnp.where(c == 31, blank, sb[pl.ds(17 * 128, 128), :])

    def match_columns(j, _):
        at = pl.multiple_of(j * 128, 128)
        three = jnp.concatenate([sb[pl.ds(at + 128 * p, 128), :] for p in range(3)], axis=1)
        matched[:, pl.ds(at, 128)] = dot(three, fcol_m[...])
        return 0

    lax.fori_loop(0, 16, match_columns, 0, unroll=4)


def on_device(exposure, offsets, fraction, route_patch, route_slot, block_weight, kernel_rows, kernel_columns):
    vmem = pl.BlockSpec(memory_space=pltpu.VMEM)
    smem = pl.BlockSpec(memory_space=pltpu.SMEM)
    dma = pltpu.SemaphoreType.DMA
    names = route_patch[0]
    block = jnp.arange(64)
    before = (names[None, :] == names[:, None]) & (block[None, :] < block[:, None])
    rank = jnp.sum(before.astype(I32), axis=1)
    target = names + N * rank
    at = (block % 32) * 2 + block // 32
    place = jnp.sum(jnp.where(jnp.arange(2 * N)[:, None] == target[None, :], at[None, :], 0), axis=1)
    return pl.pallas_call(
        kernel,
        out_shape=(
            jax.ShapeDtypeStruct((PROWS, PCOLS), BF16),
            jax.ShapeDtypeStruct((PROWS, PCOLS), F32),
        ),
        in_specs=[pl.BlockSpec(memory_space=pl.ANY), smem, smem, smem, vmem, vmem, vmem, smem, smem],
        out_specs=(vmem, vmem),
        scratch_shapes=[
            pltpu.VMEM((EXT, COLS), BF16),
            pltpu.VMEM(((TILES + 2) * 64, 128), BF16),
            pltpu.VMEM((TILES * 2, 32, 128), BF16),
            pltpu.VMEM((N, 64, 128), BF16),
            pltpu.VMEM((N, 64, 128), BF16),
            pltpu.VMEM((N * 64, 128), F32),
            pltpu.VMEM((32 * 64, 128), F32),
            pltpu.VMEM((PROWS + 2 * RIM, PCOLS + 256), BF16),
            pltpu.VMEM((18 * 128, 128), BF16),
            pltpu.VMEM((ROWS, EXT), BF16),
            pltpu.VMEM((384, 128), BF16),
            pltpu.VMEM((PROWS, PROWS + 2 * RIM), BF16),
            pltpu.VMEM((384, 128), BF16),
            pltpu.VMEM((64, 256), BF16),
            pltpu.VMEM((N, 1, 128), F32),
            dma,
            dma((4,)),
            dma((4, 3)),
            dma((4, 3)),
            dma,
            dma,
            dma((2, 8)),
        ],
        compiler_params=pltpu.CompilerParams(
            collective_id=0, has_side_effects=True, vmem_limit_bytes=40 * 2**20
        ),
    )(exposure, offsets, fraction, place, route_patch, route_slot, block_weight, kernel_rows, kernel_columns)


def solution(mesh):
    placed = (
        P("visit", "ccd", None),
        P("visit", "ccd", None),
        P("visit", "ccd", None),
        P("visit", "ccd"),
        P("visit", "ccd"),
        P("visit", "ccd"),
        P(),
        P(),
    )
    return jax.shard_map(
        on_device,
        mesh=mesh,
        in_specs=placed,
        out_specs=(P("visit", "ccd"), P("visit", "ccd")),
        check_vma=False,
    )
```

```python
import functools
import math

import jax
import jax.numpy as jnp
from jax import lax
from jax.experimental import pallas as pl
from jax.experimental.pallas import tpu as pltpu
from jax.sharding import PartitionSpec as P

MESH = pl.DeviceIdType.MESH
N = 128
ROWS = 64
COLS = 4096
EDGE = 48
EXT = ROWS + 2 * EDGE
TILES = COLS // 128
TAPS = 33
RIM = 16
PROWS, PCOLS = 128, 2048
F32, BF16, I32 = jnp.float32, jnp.bfloat16, jnp.int32


def iota(shape, dim):
    return lax.broadcasted_iota(I32, shape, dim)


def dot(a, b):
    return jnp.dot(a, b, preferred_element_type=F32)


def sinc(t):
    x = math.pi * t
    zero = t == 0.0
    x = jnp.where(zero, 1.0, x)
    return jnp.where(zero, 1.0, jnp.sin(x) / x)


def lanczos(f):
    k = iota((8, 128), 0)
    t = (3 - k).astype(F32) - f
    w = jnp.where(k < 6, sinc(t) * sinc(t / 3.0), 0.0)
    return w / jnp.sum(w, axis=0, keepdims=True)


def band(lag, weights):
    m = jnp.zeros(lag.shape, F32)
    for k, w in enumerate(weights):
        m = jnp.where(lag == k, w, m)
    return m


def kernel(
    exposure, offsets_h, fraction_h, patch_h, slot_h, weight_h, krows_h, kcols_h,
    fr_h, frow_h, fcol_h,
    ext, rwb, wb, sbuf, rbuf, gf, nf, fr, row_m, col_m, frow_m, fcol_m, a_m, meta, offsets, fraction, route_patch, route_slot, block_weight, kernel_rows, kernel_columns, idx_v, idx_s,
    sem_in, sem_small, sem_mg, sem_meta, sem_s, sem_r, sem_rim, sem_out,
):
    v = lax.axis_index("visit")
    c = lax.axis_index("ccd")
    me = v * 32 + c
    core = lax.rem(c, 2)
    z = lax.rem(c // 2, 4)
    x = c // 8

    def peer(dv, dx, dz, dc):
        return (
            lax.rem(v + dv, 4),
            (lax.rem(x + dx, 4) * 4 + lax.rem(z + dz, 4)) * 2 + lax.rem(core + dc, 2),
        )

    def remote(src, dst, s, r, to):
        return pltpu.make_async_remote_copy(
            src_ref=src, dst_ref=dst, send_sem=s, recv_sem=r, device_id=to, device_id_type=MESH
        )

    c_next, c_prev = lax.rem(c + 1, 32), lax.rem(c + 31, 32)
    v_next, v_prev = lax.rem(v + 1, 4), lax.rem(v + 3, 4)

    bar = pltpu.get_barrier_semaphore()
    plane = [peer(0, i // 4, i % 4, 0) for i in range(1, 16)]
    line = [peer(i // 2, 0, 0, i % 2) for i in range(1, 8)]
    first = [(v, c_next), (v, c_prev)] + plane + line
    for to in first:
        pl.semaphore_signal(bar, inc=1, device_id=to, device_id_type=MESH)

    own = pltpu.make_async_copy(exposure.at[0], ext.at[pl.ds(EDGE, ROWS)], sem_in)
    own.start()
    small = [
        pltpu.make_async_copy(there, here, sem_small.at[n])
        for n, (there, here) in enumerate(
            (
                (patch_h, route_patch), (slot_h, route_slot), (weight_h, block_weight), (offsets_h, offsets),
                (fraction_h, fraction), (krows_h, kernel_rows), (kcols_h, kernel_columns),
            )
        )
    ]
    for copy in small:
        copy.start()
    for copy in small:
        copy.wait()

    dest_r = jnp.broadcast_to(route_patch[...], (64, 64))
    eye = iota((64, 64), 0) == iota((64, 64), 1)
    dest_c = jnp.sum(jnp.where(eye, dest_r, 0), axis=1, keepdims=True)
    before = (dest_r == dest_c) & (iota((64, 64), 1) < iota((64, 64), 0))
    rank_c = jnp.sum(jnp.where(before, 1, 0), axis=1, keepdims=True)
    b_c = iota((64, 128), 0)
    place = jnp.where(b_c < 32, 2 * b_c, 2 * b_c - 63)
    names = dest_c == iota((64, 128), 1)
    for k in range(2):
        chosen = jnp.where(names & (rank_c == k), place, 0)
        idx_v[pl.ds(k, 1), :] = jnp.sum(chosen, axis=0, keepdims=True)
    to_smem = pltpu.make_async_copy(idx_v, idx_s, sem_small.at[7])
    to_smem.start()

    code = (route_patch[...] * 64 + route_slot[...]).astype(F32)
    mine = v * 32 + core * 16 + x * 4 + z
    meta[mine] = jnp.concatenate([code, block_weight[...].astype(F32)], axis=1)

    pl.semaphore_wait(bar, len(first))

    margins = [
        remote(exposure.at[0, pl.ds(ROWS - EDGE, EDGE)], ext.at[pl.ds(0, EDGE)], sem_mg.at[0], sem_mg.at[1], (v, c_next)),
        remote(exposure.at[0, pl.ds(0, EDGE)], ext.at[pl.ds(EDGE + ROWS, EDGE)], sem_mg.at[2], sem_mg.at[3], (v, c_prev)),
    ]

    def stage(start, rows, peers, at):
        piece = meta.at[pl.ds(start, rows)]
        copies = [remote(piece, piece, sem_meta.at[0, at + i], sem_meta.at[1, at + i], to) for i, to in enumerate(peers)]
        for copy in copies:
            copy.start()
        return copies

    def finish(copies):
        for copy in copies:
            copy.wait()

    going = stage(mine, 1, plane, 0)
    for copy in margins:
        copy.start()
    w_row = lanczos(fraction[0, 0, 0]).astype(BF16).astype(F32)
    r = iota((ROWS, EXT), 0)
    row = jnp.where((r >= 16) & (r < 32), r + 16, jnp.where((r >= 32) & (r < 48), r - 16, r))
    lag = iota((ROWS, EXT), 1) - row - (EDGE - 3 - offsets[0, 0, 0])
    m = band(lag, [w_row[k : k + 1, 0:1] for k in range(6)])
    at = iota((ROWS, EXT), 1)
    outside = ((at < EDGE) & (c == 0)) | ((at >= EDGE + ROWS) & (c == 31))
    row_m[...] = jnp.where(outside, 0.0, m).astype(BF16)

    w_col = lanczos(fraction[0, 0, 1]).astype(BF16).astype(F32)
    lag = iota((384, 128), 0) - iota((384, 128), 1) - (125 - offsets[0, 0, 1])
    col_m[...] = band(lag, [w_col[k : k + 1, 0:1] for k in range(6)]).astype(BF16)
    finish(going)
    going = stage(v * 32 + core * 16, 16, line, 15)
    blank = jnp.zeros((64, 128), BF16)
    rwb[0] = blank
    rwb[TILES + 1] = blank
    own.wait()
    for copy in margins:
        copy.wait()

    def row_pass(i, _):
        got = dot(row_m[...], ext[:, pl.ds(pl.multiple_of(i * 256, 256), 256)]).astype(BF16)
        rwb[2 * i + 1] = got[:, :128]
        rwb[2 * i + 2] = got[:, 128:]
        return 0

    lax.fori_loop(0, TILES // 2, row_pass, 0, unroll=4)

    def column_pass(half, i, _):
        parts = [rwb[pl.ds(i * 8 + p, 8), pl.ds(32 * half, 32), :].reshape(256, 128) for p in range(3)]
        got = dot(jnp.concatenate(parts, axis=1), col_m[...]).astype(BF16)
        wb[half, pl.ds(i * 16, 16)] = got.reshape(16, 16, 128)
        return 0

    def pick(half, p, out, o):
        for k in range(2):
            out[half, o, pl.ds(16 * k, 16), :] = wb[half, idx_s[k, p]]

    def send(half, d, _):
        e = lax.rem(d * 37, N)
        pv, pc = peer(e // 32, lax.rem(e // 8, 4), lax.rem(e // 2, 4), lax.rem(e, 2))
        pick(half, pv * 32 + pc, sbuf, d)
        remote(sbuf.at[half, d], rbuf.at[half, me], sem_s.at[half], sem_r.at[half], (pv, pc)).start()
        return 0

    for half in range(2):
        lax.fori_loop(0, TILES // 8, functools.partial(column_pass, half), 0, unroll=2)
        if half == 0:
            to_smem.wait()
            finish(going)
        lax.fori_loop(1, N, functools.partial(send, half), 0)
        pick(half, me, rbuf, me)

    lag = iota((PROWS, PROWS + 2 * RIM), 1) - iota((PROWS, PROWS + 2 * RIM), 0)
    m = band(lag, [kernel_rows[k] for k in range(TAPS)])
    at = iota((PROWS, PROWS + 2 * RIM), 1)
    outside = ((at < RIM) & (v == 0)) | ((at >= RIM + PROWS) & (v == 3))
    frow_m[...] = jnp.where(outside, 0.0, m).astype(BF16)
    lag = iota((384, 128), 0) - iota((384, 128), 1) - (128 - RIM)
    fcol_m[...] = band(lag, [kernel_columns[k] for k in range(TAPS)]).astype(BF16)
    outs = [pltpu.make_async_copy(frow_m, frow_h, sem_out.at[0]), pltpu.make_async_copy(fcol_m, fcol_h, sem_out.at[1])]
    for copy in outs:
        copy.start()

    every = meta[:, 0, :]
    s_to = iota((N, N), 0)
    s_from = (s_to // 32) * 32 + (s_to % 2) * 16 + (s_to % 32) // 2
    swap = jnp.where(s_from == iota((N, N), 1), 1.0, 0.0).astype(BF16)
    weight = pltpu.roll(every, 64, 1)
    patch = jnp.floor(every * (1.0 / 64.0))
    slot = every - patch * 64.0
    lane = iota((N, N), 1)
    match = (patch == me.astype(F32)) & (lane < 64)
    earlier = jnp.where(iota((N, N), 0) < iota((N, N), 1), 1.0, 0.0).astype(BF16)
    rank = dot(jnp.where(match, 1.0, 0.0).astype(BF16), earlier)
    total = jnp.zeros((64, 1), F32)
    for k in range(2):
        chosen = match & (rank == float(k))
        s_k = jnp.sum(jnp.where(chosen, slot, 0.0), axis=1, keepdims=True)
        w_k = jnp.sum(jnp.where(chosen, weight, 0.0), axis=1, keepdims=True)
        table = dot(swap, jnp.where(lane.astype(F32) == s_k, w_k, 0.0).astype(BF16)).T[:64]
        total = total + jnp.sum(table, axis=1, keepdims=True)
        a_m[:, pl.ds(128 * k, 128)] = table.astype(BF16)
    scale = 1.0 / jnp.maximum(total, 1.0)

    top, bottom, centre = pl.ds(RIM, RIM), pl.ds(PROWS, RIM), pl.ds(RIM, PROWS)
    above, below = pl.ds(0, RIM), pl.ds(RIM + PROWS, RIM)
    west, east, across = pl.ds(128, 128), pl.ds(PCOLS, 128), pl.ds(128, PCOLS)
    left, right = pl.ds(0, 128), pl.ds(128 + PCOLS, 128)
    rims = [
        remote(fr.at[rows, cols], fr.at[to_rows, to_cols], sem_rim.at[0, n], sem_rim.at[1, n], to)
        for n, (rows, cols, to_rows, to_cols, to) in enumerate(
            (
                (top, across, below, across, (v_prev, c)),
                (top, east, below, left, (v_prev, c_next)),
                (top, west, below, right, (v_prev, c_prev)),
                (bottom, across, above, across, (v_next, c)),
                (centre, east, centre, left, (v, c_next)),
                (centre, west, centre, right, (v, c_prev)),
                (bottom, east, above, left, (v_next, c_next)),
                (bottom, west, above, right, (v_next, c_prev)),
            )
        )
    ]

    def widen(half, s, _):
        gf[pl.ds(pl.multiple_of(s * 32, 32), 32), :] = rbuf[half, s].astype(F32)
        return 0

    def coadd(i, _):
        pair = []
        for y in (2 * i, 2 * i + 1):
            halves = [gf[pl.ds(16 * k + y, N, stride=32), :] for k in range(2)]
            pair.append(jnp.concatenate(halves, axis=0).astype(BF16))
        got = dot(a_m[...], jnp.concatenate(pair, axis=1)) * scale
        nf[pl.ds(pl.multiple_of(i * 128, 128), 64), :] = got[:, :128]
        nf[pl.ds(pl.multiple_of(i * 128 + 64, 64), 64), :] = got[:, 128:]
        return 0

    def lay(half, j, _):
        at = pl.multiple_of(j * 128, 128)
        for i in range(4):
            tile = nf[pl.ds(i * 16 + j, 16, stride=64), :].astype(BF16)
            fr[pl.ds(RIM + 32 * i + 16 * half, 16), pl.ds(at + 128, 128)] = tile
        return 0

    for half in range(2):
        sent = sbuf.at[half, pl.ds(1, N - 1)]
        pltpu.make_async_copy(sent, sent, sem_r.at[half]).wait()
        lax.fori_loop(0, N, functools.partial(widen, half), 0, unroll=8)
        lax.fori_loop(0, 8, coadd, 0, unroll=4)
        lax.fori_loop(0, 16, functools.partial(lay, half), 0, unroll=4)
        for copy in rims[3 * half : 3 + 5 * half]:
            copy.start()

    for half in range(2):
        sent = sbuf.at[half, pl.ds(1, N - 1)]
        pltpu.make_async_copy(sent, sent, sem_s.at[half]).wait()
    for copy in rims:
        copy.wait()
    outs.append(pltpu.make_async_copy(fr, fr_h, sem_out.at[2]))
    outs[2].start()
    for copy in outs:
        copy.wait()


def filter_kernel(fr, frow_m, fcol_m, coadded, matched, sb, out, sem):
    c = lax.axis_index("ccd")
    lower = pltpu.make_async_copy(fr.at[pl.ds(RIM, PROWS), pl.ds(128, PCOLS)], coadded, sem.at[0])
    lower.start()

    def smooth(i, _):
        got = dot(frow_m[...], fr[:, pl.ds(pl.multiple_of(i * 256, 256), 256)]).astype(BF16)
        at = pl.multiple_of(i * 256, 256)
        sb[pl.ds(at, 128), :] = got[:, :128]
        sb[pl.ds(at + 128, 128), :] = got[:, 128:]
        return 0

    lax.fori_loop(0, 9, smooth, 0, unroll=3)
    blank = jnp.zeros((128, 128), BF16)
    sb[pl.ds(0, 128), :] = jnp.where(c == 0, blank, sb[pl.ds(0, 128), :])
    sb[pl.ds(17 * 128, 128), :] = jnp.where(c == 31, blank, sb[pl.ds(17 * 128, 128), :])

    copies = []
    for half in range(2):
        for j in range(8 * half, 8 * half + 8):
            three = jnp.concatenate([sb[pl.ds((j + p) * 128, 128), :] for p in range(3)], axis=1)
            out[:, pl.ds(j * 128, 128)] = dot(three, fcol_m[...])
        cols = pl.ds(half * 1024, 1024)
        copies.append(pltpu.make_async_copy(out.at[:, cols], matched.at[:, cols], sem.at[1 + half]))
        copies[-1].start()
    for copy in [lower] + copies:
        copy.wait()


def on_device(exposure, offsets, fraction, route_patch, route_slot, block_weight, kernel_rows, kernel_columns):
    hbm = pl.BlockSpec(memory_space=pltpu.HBM)
    vmem = pl.BlockSpec(memory_space=pltpu.VMEM)
    dma = pltpu.SemaphoreType.DMA
    framed = pl.pallas_call(
        kernel,
        out_shape=(
            jax.ShapeDtypeStruct((PROWS + 2 * RIM, PCOLS + 256), BF16),
            jax.ShapeDtypeStruct((PROWS, PROWS + 2 * RIM), BF16),
            jax.ShapeDtypeStruct((384, 128), BF16),
        ),
        in_specs=[hbm] * 8,
        out_specs=(hbm,) * 3,
        scratch_shapes=[
            pltpu.VMEM((EXT, COLS), BF16),
            pltpu.VMEM((TILES + 2, 64, 128), BF16),
            pltpu.VMEM((2, TILES * 2, 16, 128), BF16),
            pltpu.VMEM((2, N, 32, 128), BF16),
            pltpu.VMEM((2, N, 32, 128), BF16),
            pltpu.VMEM((N * 32, 128), F32),
            pltpu.VMEM((16 * 64, 128), F32),
            pltpu.VMEM((PROWS + 2 * RIM, PCOLS + 256), BF16),
            pltpu.VMEM((ROWS, EXT), BF16),
            pltpu.VMEM((384, 128), BF16),
            pltpu.VMEM((PROWS, PROWS + 2 * RIM), BF16),
            pltpu.VMEM((384, 128), BF16),
            pltpu.VMEM((64, 256), BF16),
            pltpu.VMEM((N, 1, 128), F32),
            pltpu.SMEM((1, 1, 2), I32),
            pltpu.SMEM((1, 1, 2), F32),
            pltpu.VMEM((1, 64), I32),
            pltpu.VMEM((1, 64), I32),
            pltpu.VMEM((1, 64), BF16),
            pltpu.SMEM((TAPS,), F32),
            pltpu.SMEM((TAPS,), F32),
            pltpu.VMEM((2, 128), I32),
            pltpu.SMEM((2, 128), I32),
            dma,
            dma((8,)),
            dma((4,)),
            dma((2, 22)),
            dma((2,)),
            dma((2,)),
            dma((2, 8)),
            dma((3,)),
        ],
        compiler_params=pltpu.CompilerParams(
            collective_id=0, has_side_effects=True, vmem_limit_bytes=60 * 2**20
        ),
    )(exposure, offsets, fraction, route_patch, route_slot, block_weight, kernel_rows, kernel_columns)
    return pl.pallas_call(
        filter_kernel,
        out_shape=(
            jax.ShapeDtypeStruct((PROWS, PCOLS), BF16),
            jax.ShapeDtypeStruct((PROWS, PCOLS), F32),
        ),
        in_specs=[vmem] * 3,
        out_specs=(hbm, hbm),
        scratch_shapes=[
            pltpu.VMEM((18 * 128, 128), BF16),
            pltpu.VMEM((PROWS, PCOLS), F32),
            dma((3,)),
        ],
        compiler_params=pltpu.CompilerParams(vmem_limit_bytes=60 * 2**20),
    )(*framed)


def solution(mesh):
    placed = (
        P("visit", "ccd", None),
        P("visit", "ccd", None),
        P("visit", "ccd", None),
        P("visit", "ccd"),
        P("visit", "ccd"),
        P("visit", "ccd"),
        P(),
        P(),
    )
    return jax.shard_map(
        on_device,
        mesh=mesh,
        in_specs=placed,
        out_specs=(P("visit", "ccd"), P("visit", "ccd")),
        check_vma=False,
    )
```

```python
import functools
import math

import jax
import jax.numpy as jnp
from jax import lax
from jax.experimental import pallas as pl
from jax.experimental.pallas import tpu as pltpu
from jax.sharding import PartitionSpec as P

MESH = pl.DeviceIdType.MESH
N = 128
ROWS = 64
COLS = 4096
EDGE = 48
EXT = ROWS + 2 * EDGE
TILES = COLS // 128
TAPS = 33
PARTS = 4
RIM = 16
PROWS, PCOLS = 128, 2048
F32, BF16, I32 = jnp.float32, jnp.bfloat16, jnp.int32


def iota(shape, dim):
    return lax.broadcasted_iota(I32, shape, dim)


def dot(a, b):
    return jnp.dot(a, b, preferred_element_type=F32)


def sinc(t):
    x = math.pi * t
    zero = t == 0.0
    x = jnp.where(zero, 1.0, x)
    return jnp.where(zero, 1.0, jnp.sin(x) / x)


def lanczos(f):
    k = iota((8, 128), 0)
    t = (3 - k).astype(F32) - f
    w = jnp.where(k < 6, sinc(t) * sinc(t / 3.0), 0.0)
    return w / jnp.sum(w, axis=0, keepdims=True)


def band(lag, weights):
    m = jnp.zeros(lag.shape, F32)
    for k, w in enumerate(weights):
        m = jnp.where(lag == k, w, m)
    return m


def kernel(
    exposure, offsets_h, fraction_h, patch_h, slot_h, weight_h, krows_h, kcols_h,
    fr_h, frow_h, fcol_h,
    ext, rwb, wb, sbuf, rbuf, gf, nf, fr, row_m, col_m, frow_m, fcol_m, a_m, meta, offsets, fraction, route_patch, route_slot, block_weight, kernel_rows, kernel_columns, idx_v, idx_s,
    sem_in, sem_small, sem_mg, sem_round, sem_meta, sem_s, sem_r, sem_rim, sem_out,
):
    v = lax.axis_index("visit")
    c = lax.axis_index("ccd")
    me = v * 32 + c
    core = lax.rem(c, 2)
    z = lax.rem(c // 2, 4)
    x = c // 8

    def peer(dv, dx, dz, dc):
        return (
            lax.rem(v + dv, 4),
            (lax.rem(x + dx, 4) * 4 + lax.rem(z + dz, 4)) * 2 + lax.rem(core + dc, 2),
        )

    def remote(src, dst, s, r, to):
        return pltpu.make_async_remote_copy(
            src_ref=src, dst_ref=dst, send_sem=s, recv_sem=r, device_id=to, device_id_type=MESH
        )

    c_next, c_prev = lax.rem(c + 1, 32), lax.rem(c + 31, 32)
    v_next, v_prev = lax.rem(v + 1, 4), lax.rem(v + 3, 4)

    bar = pltpu.get_barrier_semaphore()
    plane = [peer(0, i // 4, i % 4, 0) for i in range(1, 16)]
    line = [peer(i // 2, 0, 0, i % 2) for i in range(1, 8)]
    first = [(v, c_next), (v, c_prev)] + plane + line
    for to in first:
        pl.semaphore_signal(bar, inc=1, device_id=to, device_id_type=MESH)

    own = pltpu.make_async_copy(exposure.at[0], ext.at[pl.ds(EDGE, ROWS)], sem_in)
    own.start()
    small = [
        pltpu.make_async_copy(there, here, sem_small.at[n])
        for n, (there, here) in enumerate(
            (
                (patch_h, route_patch), (slot_h, route_slot), (weight_h, block_weight), (offsets_h, offsets),
                (fraction_h, fraction), (krows_h, kernel_rows), (kcols_h, kernel_columns),
            )
        )
    ]
    for copy in small:
        copy.start()
    pl.semaphore_wait(bar, len(first))
    for to in line:
        pl.semaphore_signal(sem_round, inc=1, device_id=to, device_id_type=MESH)

    margins = []
    for n in range(PARTS):
        cols = pl.ds(n * (COLS // PARTS), COLS // PARTS)
        low, high = exposure.at[0, pl.ds(ROWS - EDGE, EDGE), cols], exposure.at[0, pl.ds(0, EDGE), cols]
        margins.append(
            [
                remote(low, ext.at[pl.ds(0, EDGE), cols], sem_mg.at[0, n], sem_mg.at[1, n], (v, c_next)),
                remote(high, ext.at[pl.ds(EDGE + ROWS, EDGE), cols], sem_mg.at[2, n], sem_mg.at[3, n], (v, c_prev)),
            ]
        )

    for pair in margins:
        for copy in pair:
            copy.start()

    for copy in small:
        copy.wait()

    code = (route_patch[...] * 64 + route_slot[...]).astype(F32)
    meta[me] = jnp.concatenate([code, block_weight[...].astype(F32)], axis=1)

    w_row = lanczos(fraction[0, 0, 0]).astype(BF16).astype(F32)
    r = iota((ROWS, EXT), 0)
    row = jnp.where((r >= 16) & (r < 32), r + 16, jnp.where((r >= 32) & (r < 48), r - 16, r))
    lag = iota((ROWS, EXT), 1) - row - (EDGE - 3 - offsets[0, 0, 0])
    m = band(lag, [w_row[k : k + 1, 0:1] for k in range(6)])
    at = iota((ROWS, EXT), 1)
    outside = ((at < EDGE) & (c == 0)) | ((at >= EDGE + ROWS) & (c == 31))
    row_m[...] = jnp.where(outside, 0.0, m).astype(BF16)

    w_col = lanczos(fraction[0, 0, 1]).astype(BF16).astype(F32)
    lag = iota((384, 128), 0) - iota((384, 128), 1) - (125 - offsets[0, 0, 1])
    col_m[...] = band(lag, [w_col[k : k + 1, 0:1] for k in range(6)]).astype(BF16)
    dest_r = jnp.broadcast_to(route_patch[...], (64, 64))
    eye = iota((64, 64), 0) == iota((64, 64), 1)
    dest_c = jnp.sum(jnp.where(eye, dest_r, 0), axis=1, keepdims=True)
    before = (dest_r == dest_c) & (iota((64, 64), 1) < iota((64, 64), 0))
    rank_c = jnp.sum(jnp.where(before, 1, 0), axis=1, keepdims=True)
    b_c = iota((64, 128), 0)
    place = jnp.where(b_c < 32, 2 * b_c, 2 * b_c - 63)
    names = dest_c == iota((64, 128), 1)
    for k in range(2):
        chosen = jnp.where(names & (rank_c == k), place, 0)
        idx_v[pl.ds(k, 1), :] = jnp.sum(chosen, axis=0, keepdims=True)
    to_smem = pltpu.make_async_copy(idx_v, idx_s, sem_small.at[7])
    to_smem.start()

    blank = jnp.zeros((64, 128), BF16)
    rwb[0] = blank
    rwb[TILES + 1] = blank
    own.wait()

    def row_pass(i, _):
        got = dot(row_m[...], ext[:, pl.ds(pl.multiple_of(i * 256, 256), 256)]).astype(BF16)
        rwb[2 * i + 1] = got[:, :128]
        rwb[2 * i + 2] = got[:, 128:]
        return 0

    for n, pair in enumerate(margins):
        for copy in pair:
            copy.wait()
        per = TILES // 2 // PARTS
        lax.fori_loop(n * per, (n + 1) * per, row_pass, 0, unroll=4)

    def column_pass(half, i, _):
        parts = [rwb[pl.ds(i * 8 + p, 8), pl.ds(32 * half, 32), :].reshape(256, 128) for p in range(3)]
        got = dot(jnp.concatenate(parts, axis=1), col_m[...]).astype(BF16)
        wb[half, pl.ds(i * 16, 16)] = got.reshape(16, 16, 128)
        return 0

    def pick(half, p, out, o):
        for k in range(2):
            out[half, o, pl.ds(16 * k, 16), :] = wb[half, idx_s[k, p]]

    def send(half, d, _):
        e = lax.rem(d * 53, N)
        pv, pc = peer(e // 32, lax.rem(e // 8, 4), lax.rem(e // 2, 4), lax.rem(e, 2))
        pick(half, pv * 32 + pc, sbuf, d)
        remote(sbuf.at[half, d], rbuf.at[half, me], sem_s.at[half], sem_r.at[half], (pv, pc)).start()
        if half == 0:
            remote(meta.at[me], meta.at[me], sem_meta.at[0], sem_meta.at[1], (pv, pc)).start()
        return 0

    for half in range(2):
        lax.fori_loop(0, TILES // 8, functools.partial(column_pass, half), 0, unroll=2)
        if half == 0:
            to_smem.wait()
            pl.semaphore_wait(sem_round, len(line))
        lax.fori_loop(1, N, functools.partial(send, half), 0)
        pick(half, me, rbuf, me)

    lag = iota((PROWS, PROWS + 2 * RIM), 1) - iota((PROWS, PROWS + 2 * RIM), 0)
    m = band(lag, [kernel_rows[k] for k in range(TAPS)])
    at = iota((PROWS, PROWS + 2 * RIM), 1)
    outside = ((at < RIM) & (v == 0)) | ((at >= RIM + PROWS) & (v == 3))
    frow_m[...] = jnp.where(outside, 0.0, m).astype(BF16)
    lag = iota((384, 128), 0) - iota((384, 128), 1) - (128 - RIM)
    fcol_m[...] = band(lag, [kernel_columns[k] for k in range(TAPS)]).astype(BF16)
    outs = [pltpu.make_async_copy(frow_m, frow_h, sem_out.at[0]), pltpu.make_async_copy(fcol_m, fcol_h, sem_out.at[1])]
    for copy in outs:
        copy.start()

    for i in range(2):
        pltpu.make_async_copy(meta.at[pl.ds(0, N - 1)], meta.at[pl.ds(0, N - 1)], sem_meta.at[i]).wait()
    every = meta[:, 0, :]
    weight = pltpu.roll(every, 64, 1)
    patch = jnp.floor(every * (1.0 / 64.0))
    slot = every - patch * 64.0
    lane = iota((N, N), 1)
    match = (patch == me.astype(F32)) & (lane < 64)
    earlier = jnp.where(iota((N, N), 0) < iota((N, N), 1), 1.0, 0.0).astype(BF16)
    rank = dot(jnp.where(match, 1.0, 0.0).astype(BF16), earlier)
    total = jnp.zeros((64, 1), F32)
    for k in range(2):
        chosen = match & (rank == float(k))
        s_k = jnp.sum(jnp.where(chosen, slot, 0.0), axis=1, keepdims=True)
        w_k = jnp.sum(jnp.where(chosen, weight, 0.0), axis=1, keepdims=True)
        table = jnp.where(lane.astype(F32) == s_k, w_k, 0.0).T[:64]
        total = total + jnp.sum(table, axis=1, keepdims=True)
        a_m[:, pl.ds(128 * k, 128)] = table.astype(BF16)
    scale = 1.0 / jnp.maximum(total, 1.0)

    top, bottom, centre = pl.ds(RIM, RIM), pl.ds(PROWS, RIM), pl.ds(RIM, PROWS)
    above, below = pl.ds(0, RIM), pl.ds(RIM + PROWS, RIM)
    west, east, across = pl.ds(128, 128), pl.ds(PCOLS, 128), pl.ds(128, PCOLS)
    left, right = pl.ds(0, 128), pl.ds(128 + PCOLS, 128)
    rims = [
        remote(fr.at[rows, cols], fr.at[to_rows, to_cols], sem_rim.at[0, n], sem_rim.at[1, n], to)
        for n, (rows, cols, to_rows, to_cols, to) in enumerate(
            (
                (top, across, below, across, (v_prev, c)),
                (top, east, below, left, (v_prev, c_next)),
                (top, west, below, right, (v_prev, c_prev)),
                (bottom, across, above, across, (v_next, c)),
                (centre, east, centre, left, (v, c_next)),
                (centre, west, centre, right, (v, c_prev)),
                (bottom, east, above, left, (v_next, c_next)),
                (bottom, west, above, right, (v_next, c_prev)),
            )
        )
    ]

    def widen(half, s, _):
        gf[pl.ds(pl.multiple_of(s * 40, 8), 32), :] = rbuf[half, s].astype(F32)
        return 0

    def coadd(i, _):
        pair = []
        for y in (2 * i, 2 * i + 1):
            halves = [gf[pl.ds(16 * k + y, N, stride=40), :] for k in range(2)]
            pair.append(jnp.concatenate(halves, axis=0).astype(BF16))
        got = dot(a_m[...], jnp.concatenate(pair, axis=1)) * scale
        nf[pl.ds(pl.multiple_of(i * 144, 8), 64), :] = got[:, :128]
        nf[pl.ds(pl.multiple_of(i * 144 + 72, 8), 64), :] = got[:, 128:]
        return 0

    def lay(half, j, _):
        at = pl.multiple_of(j * 128, 128)
        for i in range(4):
            tile = nf[pl.ds(i * 16 + j, 16, stride=72), :].astype(BF16)
            fr[pl.ds(RIM + 32 * i + 16 * half, 16), pl.ds(at + 128, 128)] = tile
        return 0

    for half in range(2):
        sent = sbuf.at[half, pl.ds(1, N - 1)]
        pltpu.make_async_copy(sent, sent, sem_r.at[half]).wait()
        lax.fori_loop(0, N, functools.partial(widen, half), 0, unroll=8)
        lax.fori_loop(0, 8, coadd, 0, unroll=4)
        lax.fori_loop(0, 16, functools.partial(lay, half), 0, unroll=4)
        for copy in rims[3 * half : 3 + 5 * half]:
            copy.start()

    for half in range(2):
        sent = sbuf.at[half, pl.ds(1, N - 1)]
        pltpu.make_async_copy(sent, sent, sem_s.at[half]).wait()
    everywhere = pl.ds(0, PCOLS + 256)
    parts = ((centre, across), (above, everywhere), (below, everywhere), (centre, left), (centre, right))
    for n, where in enumerate(parts):
        outs.append(pltpu.make_async_copy(fr.at[where], fr_h.at[where], sem_out.at[2 + n]))
    outs[2].start()
    for copy in rims:
        copy.wait()
    for copy in outs[3:]:
        copy.start()
    for copy in outs:
        copy.wait()


def filter_kernel(fr_h, frow_h, fcol_h, coadded, matched, fr, frow_m, fcol_m, sb, out, sem):
    c = lax.axis_index("ccd")
    ins = [pltpu.make_async_copy(frow_h, frow_m, sem.at[0]), pltpu.make_async_copy(fcol_h, fcol_m, sem.at[1])]
    for n in range(3):
        cols = pl.ds(n * 768, 768)
        ins.append(pltpu.make_async_copy(fr_h.at[:, cols], fr.at[:, cols], sem.at[2 + n]))
    for copy in ins:
        copy.start()
    outs = []
    ins[0].wait()
    ins[1].wait()

    done = 0
    for n in range(3):
        ins[2 + n].wait()
        left, right = max(768 * n, 128), min(768 * n + 768, 128 + PCOLS)
        centre = fr.at[pl.ds(RIM, PROWS), pl.ds(left, right - left)]
        outs.append(pltpu.make_async_copy(centre, coadded.at[:, pl.ds(left - 128, right - left)], sem.at[5 + n]))
        outs[-1].start()
        for i in range(3 * n, 3 * n + 3):
            got = dot(frow_m[...], fr[:, pl.ds(i * 256, 256)]).astype(BF16)
            for half in range(2):
                tile = got[:, 128 * half : 128 * half + 128]
                if i == 0 and half == 0:
                    tile = jnp.where(c == 0, jnp.zeros_like(tile), tile)
                if i == 8 and half == 1:
                    tile = jnp.where(c == 31, jnp.zeros_like(tile), tile)
                sb[pl.ds(i * 256 + half * 128, 128), :] = tile
        ready = 6 * n + 4
        for j in range(done, ready):
            three = jnp.concatenate([sb[pl.ds((j + p) * 128, 128), :] for p in range(3)], axis=1)
            out[:, pl.ds(j * 128, 128)] = dot(three, fcol_m[...])
        cols = pl.ds(done * 128, (ready - done) * 128)
        outs.append(pltpu.make_async_copy(out.at[:, cols], matched.at[:, cols], sem.at[8 + n]))
        outs[-1].start()
        done = ready
    for copy in outs:
        copy.wait()


def on_device(exposure, offsets, fraction, route_patch, route_slot, block_weight, kernel_rows, kernel_columns):
    hbm = pl.BlockSpec(memory_space=pltpu.HBM)
    dma = pltpu.SemaphoreType.DMA
    framed = pl.pallas_call(
        kernel,
        out_shape=(
            jax.ShapeDtypeStruct((PROWS + 2 * RIM, PCOLS + 256), BF16),
            jax.ShapeDtypeStruct((PROWS, PROWS + 2 * RIM), BF16),
            jax.ShapeDtypeStruct((384, 128), BF16),
        ),
        in_specs=[hbm] * 8,
        out_specs=(hbm,) * 3,
        scratch_shapes=[
            pltpu.VMEM((EXT, COLS), BF16),
            pltpu.VMEM((TILES + 2, 64, 128), BF16),
            pltpu.VMEM((2, TILES * 2, 16, 128), BF16),
            pltpu.VMEM((2, N, 32, 128), BF16),
            pltpu.VMEM((2, N, 32, 128), BF16),
            pltpu.VMEM((N * 40, 128), F32),
            pltpu.VMEM((16 * 72, 128), F32),
            pltpu.VMEM((PROWS + 2 * RIM, PCOLS + 256), BF16),
            pltpu.VMEM((ROWS, EXT), BF16),
            pltpu.VMEM((384, 128), BF16),
            pltpu.VMEM((PROWS, PROWS + 2 * RIM), BF16),
            pltpu.VMEM((384, 128), BF16),
            pltpu.VMEM((64, 256), BF16),
            pltpu.VMEM((N, 1, 128), F32),
            pltpu.SMEM((1, 1, 2), I32),
            pltpu.SMEM((1, 1, 2), F32),
            pltpu.VMEM((1, 64), I32),
            pltpu.VMEM((1, 64), I32),
            pltpu.VMEM((1, 64), BF16),
            pltpu.SMEM((TAPS,), F32),
            pltpu.SMEM((TAPS,), F32),
            pltpu.VMEM((2, 128), I32),
            pltpu.SMEM((2, 128), I32),
            dma,
            dma((8,)),
            dma((4, PARTS)),
            pltpu.SemaphoreType.REGULAR,
            dma((2,)),
            dma((2,)),
            dma((2,)),
            dma((2, 8)),
            dma((7,)),
        ],
        compiler_params=pltpu.CompilerParams(
            collective_id=0, has_side_effects=True, vmem_limit_bytes=60 * 2**20
        ),
    )(exposure, offsets, fraction, route_patch, route_slot, block_weight, kernel_rows, kernel_columns)
    return pl.pallas_call(
        filter_kernel,
        out_shape=(
            jax.ShapeDtypeStruct((PROWS, PCOLS), BF16),
            jax.ShapeDtypeStruct((PROWS, PCOLS), F32),
        ),
        in_specs=[hbm] * 3,
        out_specs=(hbm, hbm),
        scratch_shapes=[
            pltpu.VMEM((PROWS + 2 * RIM, PCOLS + 256), BF16),
            pltpu.VMEM((PROWS, PROWS + 2 * RIM), BF16),
            pltpu.VMEM((384, 128), BF16),
            pltpu.VMEM((18 * 128, 128), BF16),
            pltpu.VMEM((PROWS, PCOLS), F32),
            dma((11,)),
        ],
        compiler_params=pltpu.CompilerParams(vmem_limit_bytes=60 * 2**20),
    )(*framed)


def solution(mesh):
    placed = (
        P("visit", "ccd", None),
        P("visit", "ccd", None),
        P("visit", "ccd", None),
        P("visit", "ccd"),
        P("visit", "ccd"),
        P("visit", "ccd"),
        P(),
        P(),
    )
    return jax.shard_map(
        on_device,
        mesh=mesh,
        in_specs=placed,
        out_specs=(P("visit", "ccd"), P("visit", "ccd")),
        check_vma=False,
    )
```

```python
import functools
import math

import jax
import jax.numpy as jnp
from jax import lax
from jax.experimental import pallas as pl
from jax.experimental.pallas import tpu as pltpu
from jax.sharding import PartitionSpec as P

MESH = pl.DeviceIdType.MESH
N = 128
ROWS = 64
COLS = 4096
EDGE = 48
EXT = ROWS + 2 * EDGE
TILES = COLS // 128
TAPS = 33
PARTS = 4
RIM = 16
PROWS, PCOLS = 128, 2048
F32, BF16, I32 = jnp.float32, jnp.bfloat16, jnp.int32


def iota(shape, dim):
    return lax.broadcasted_iota(I32, shape, dim)


def dot(a, b):
    return jnp.dot(a, b, preferred_element_type=F32)


def sinc(t):
    x = math.pi * t
    zero = t == 0.0
    x = jnp.where(zero, 1.0, x)
    return jnp.where(zero, 1.0, jnp.sin(x) / x)


def lanczos(f):
    k = iota((8, 128), 0)
    t = (3 - k).astype(F32) - f
    w = jnp.where(k < 6, sinc(t) * sinc(t / 3.0), 0.0)
    return w / jnp.sum(w, axis=0, keepdims=True)


def band(lag, weights):
    m = jnp.zeros(lag.shape, F32)
    for k, w in enumerate(weights):
        m = jnp.where(lag == k, w, m)
    return m


def kernel(
    exposure, offsets_h, fraction_h, patch_h, slot_h, weight_h, krows_h, kcols_h,
    fr_h, frow_h, fcol_h,
    ext, rwb, wb, sbuf, rbuf, gf, nf, fr, row_m, col_m, frow_m, fcol_m, a_m, meta, offsets, fraction, route_patch, route_slot, block_weight, kernel_rows, kernel_columns, idx_v, idx_s,
    sem_in, sem_small, sem_mg, sem_round, sem_meta, sem_s, sem_r, sem_rim, sem_out,
):
    v = lax.axis_index("visit")
    c = lax.axis_index("ccd")
    me = v * 32 + c
    core = lax.rem(c, 2)
    z = lax.rem(c // 2, 4)
    x = c // 8

    def peer(dv, dx, dz, dc):
        return (
            lax.rem(v + dv, 4),
            (lax.rem(x + dx, 4) * 4 + lax.rem(z + dz, 4)) * 2 + lax.rem(core + dc, 2),
        )

    def remote(src, dst, s, r, to):
        return pltpu.make_async_remote_copy(
            src_ref=src, dst_ref=dst, send_sem=s, recv_sem=r, device_id=to, device_id_type=MESH
        )

    c_next, c_prev = lax.rem(c + 1, 32), lax.rem(c + 31, 32)
    v_next, v_prev = lax.rem(v + 1, 4), lax.rem(v + 3, 4)

    bar = pltpu.get_barrier_semaphore()
    plane = [peer(0, i // 4, i % 4, 0) for i in range(1, 16)]
    line = [peer(i // 2, 0, 0, i % 2) for i in range(1, 8)]
    first = [(v, c_next), (v, c_prev)] + plane + line
    for to in first:
        pl.semaphore_signal(bar, inc=1, device_id=to, device_id_type=MESH)

    own = pltpu.make_async_copy(exposure.at[0], ext.at[pl.ds(EDGE, ROWS)], sem_in)
    own.start()
    small = [
        pltpu.make_async_copy(there, here, sem_small.at[n])
        for n, (there, here) in enumerate(
            (
                (patch_h, route_patch), (slot_h, route_slot), (weight_h, block_weight), (offsets_h, offsets),
                (fraction_h, fraction), (krows_h, kernel_rows), (kcols_h, kernel_columns),
            )
        )
    ]
    for copy in small:
        copy.start()
    pl.semaphore_wait(bar, len(first))
    for to in line:
        pl.semaphore_signal(sem_round, inc=1, device_id=to, device_id_type=MESH)

    margins = []
    for n in range(PARTS):
        cols = pl.ds(n * (COLS // PARTS), COLS // PARTS)
        low, high = exposure.at[0, pl.ds(ROWS - EDGE, EDGE), cols], exposure.at[0, pl.ds(0, EDGE), cols]
        margins.append(
            [
                remote(low, ext.at[pl.ds(0, EDGE), cols], sem_mg.at[0, n], sem_mg.at[1, n], (v, c_next)),
                remote(high, ext.at[pl.ds(EDGE + ROWS, EDGE), cols], sem_mg.at[2, n], sem_mg.at[3, n], (v, c_prev)),
            ]
        )

    for pair in margins:
        for copy in pair:
            copy.start()

    for copy in small:
        copy.wait()

    code = (route_patch[...] * 64 + route_slot[...]).astype(F32)
    meta[me] = jnp.concatenate([code, block_weight[...].astype(F32)], axis=1)

    w_row = lanczos(fraction[0, 0, 0]).astype(BF16).astype(F32)
    r = iota((ROWS, EXT), 0)
    row = jnp.where((r >= 16) & (r < 32), r + 16, jnp.where((r >= 32) & (r < 48), r - 16, r))
    lag = iota((ROWS, EXT), 1) - row - (EDGE - 3 - offsets[0, 0, 0])
    m = band(lag, [w_row[k : k + 1, 0:1] for k in range(6)])
    at = iota((ROWS, EXT), 1)
    outside = ((at < EDGE) & (c == 0)) | ((at >= EDGE + ROWS) & (c == 31))
    row_m[...] = jnp.where(outside, 0.0, m).astype(BF16)

    w_col = lanczos(fraction[0, 0, 1]).astype(BF16).astype(F32)
    lag = iota((384, 128), 0) - iota((384, 128), 1) - (125 - offsets[0, 0, 1])
    col_m[...] = band(lag, [w_col[k : k + 1, 0:1] for k in range(6)]).astype(BF16)
    dest_r = jnp.broadcast_to(route_patch[...], (64, 64))
    eye = iota((64, 64), 0) == iota((64, 64), 1)
    dest_c = jnp.sum(jnp.where(eye, dest_r, 0), axis=1, keepdims=True)
    before = (dest_r == dest_c) & (iota((64, 64), 1) < iota((64, 64), 0))
    rank_c = jnp.sum(jnp.where(before, 1, 0), axis=1, keepdims=True)
    b_c = iota((64, 128), 0)
    place = jnp.where(b_c < 32, 2 * b_c, 2 * b_c - 63)
    names = dest_c == iota((64, 128), 1)
    for k in range(2):
        chosen = jnp.where(names & (rank_c == k), place, 0)
        idx_v[pl.ds(k, 1), :] = jnp.sum(chosen, axis=0, keepdims=True)
    to_smem = pltpu.make_async_copy(idx_v, idx_s, sem_small.at[7])
    to_smem.start()

    blank = jnp.zeros((64, 128), BF16)
    rwb[0] = blank
    rwb[TILES + 1] = blank
    own.wait()

    def row_pass(i, _):
        got = dot(row_m[...], ext[:, pl.ds(pl.multiple_of(i * 256, 256), 256)]).astype(BF16)
        rwb[2 * i + 1] = got[:, :128]
        rwb[2 * i + 2] = got[:, 128:]
        return 0

    for n, pair in enumerate(margins):
        for copy in pair:
            copy.wait()
        per = TILES // 2 // PARTS
        lax.fori_loop(n * per, (n + 1) * per, row_pass, 0, unroll=4)

    def column_pass(half, i, _):
        parts = [rwb[pl.ds(i * 8 + p, 8), pl.ds(32 * half, 32), :].reshape(256, 128) for p in range(3)]
        got = dot(jnp.concatenate(parts, axis=1), col_m[...]).astype(BF16)
        wb[half, pl.ds(i * 16, 16)] = got.reshape(16, 16, 128)
        return 0

    def pick(half, p, out, o):
        for k in range(2):
            out[half, o, pl.ds(16 * k, 16), :] = wb[half, idx_s[k, p]]

    def send(half, d, _):
        e = lax.rem(d * 53, N)
        pv, pc = peer(e // 32, lax.rem(e // 8, 4), lax.rem(e // 2, 4), lax.rem(e, 2))
        pick(half, pv * 32 + pc, sbuf, d)
        remote(sbuf.at[half, d], rbuf.at[half, me], sem_s.at[half], sem_r.at[half], (pv, pc)).start()
        if half == 0:
            remote(meta.at[me], meta.at[me], sem_meta.at[0], sem_meta.at[1], (pv, pc)).start()
        return 0

    for half in range(2):
        lax.fori_loop(0, TILES // 8, functools.partial(column_pass, half), 0, unroll=4)
        if half == 0:
            to_smem.wait()
            pl.semaphore_wait(sem_round, len(line))
        lax.fori_loop(1, N, functools.partial(send, half), 0)
        pick(half, me, rbuf, me)

    lag = iota((PROWS, PROWS + 2 * RIM), 1) - iota((PROWS, PROWS + 2 * RIM), 0)
    m = band(lag, [kernel_rows[k] for k in range(TAPS)])
    at = iota((PROWS, PROWS + 2 * RIM), 1)
    outside = ((at < RIM) & (v == 0)) | ((at >= RIM + PROWS) & (v == 3))
    frow_m[...] = jnp.where(outside, 0.0, m).astype(BF16)
    lag = iota((384, 128), 0) - iota((384, 128), 1) - (128 - RIM)
    fcol_m[...] = band(lag, [kernel_columns[k] for k in range(TAPS)]).astype(BF16)
    outs = [pltpu.make_async_copy(frow_m, frow_h, sem_out.at[0]), pltpu.make_async_copy(fcol_m, fcol_h, sem_out.at[1])]
    for copy in outs:
        copy.start()

    for i in range(2):
        pltpu.make_async_copy(meta.at[pl.ds(0, N - 1)], meta.at[pl.ds(0, N - 1)], sem_meta.at[i]).wait()
    every = meta[:, 0, :]
    weight = pltpu.roll(every, 64, 1)
    patch = jnp.floor(every * (1.0 / 64.0))
    slot = every - patch * 64.0
    lane = iota((N, N), 1)
    match = (patch == me.astype(F32)) & (lane < 64)
    earlier = jnp.where(iota((N, N), 0) < iota((N, N), 1), 1.0, 0.0).astype(BF16)
    rank = dot(jnp.where(match, 1.0, 0.0).astype(BF16), earlier)
    total = jnp.zeros((64, 1), F32)
    for k in range(2):
        chosen = match & (rank == float(k))
        s_k = jnp.sum(jnp.where(chosen, slot, 0.0), axis=1, keepdims=True)
        w_k = jnp.sum(jnp.where(chosen, weight, 0.0), axis=1, keepdims=True)
        table = jnp.where(lane.astype(F32) == s_k, w_k, 0.0).T[:64]
        total = total + jnp.sum(table, axis=1, keepdims=True)
        a_m[:, pl.ds(128 * k, 128)] = table.astype(BF16)
    scale = 1.0 / jnp.maximum(total, 1.0)

    top, bottom, centre = pl.ds(RIM, RIM), pl.ds(PROWS, RIM), pl.ds(RIM, PROWS)
    above, below = pl.ds(0, RIM), pl.ds(RIM + PROWS, RIM)
    west, east, across = pl.ds(128, 128), pl.ds(PCOLS, 128), pl.ds(128, PCOLS)
    left, right = pl.ds(0, 128), pl.ds(128 + PCOLS, 128)
    rims = [
        remote(fr.at[rows, cols], fr.at[to_rows, to_cols], sem_rim.at[0, n], sem_rim.at[1, n], to)
        for n, (rows, cols, to_rows, to_cols, to) in enumerate(
            (
                (top, across, below, across, (v_prev, c)),
                (top, east, below, left, (v_prev, c_next)),
                (top, west, below, right, (v_prev, c_prev)),
                (bottom, across, above, across, (v_next, c)),
                (centre, east, centre, left, (v, c_next)),
                (centre, west, centre, right, (v, c_prev)),
                (bottom, east, above, left, (v_next, c_next)),
                (bottom, west, above, right, (v_next, c_prev)),
            )
        )
    ]

    def widen(half, s, _):
        gf[pl.ds(pl.multiple_of(s * 40, 8), 32), :] = rbuf[half, s].astype(F32)
        return 0

    def coadd(i, _):
        pair = []
        for y in (2 * i, 2 * i + 1):
            halves = [gf[pl.ds(16 * k + y, N, stride=40), :] for k in range(2)]
            pair.append(jnp.concatenate(halves, axis=0).astype(BF16))
        got = dot(a_m[...], jnp.concatenate(pair, axis=1)) * scale
        nf[pl.ds(pl.multiple_of(i * 144, 8), 64), :] = got[:, :128]
        nf[pl.ds(pl.multiple_of(i * 144 + 72, 8), 64), :] = got[:, 128:]
        return 0

    def lay(half, j, _):
        at = pl.multiple_of(j * 128, 128)
        for i in range(4):
            tile = nf[pl.ds(i * 16 + j, 16, stride=72), :].astype(BF16)
            fr[pl.ds(RIM + 32 * i + 16 * half, 16), pl.ds(at + 128, 128)] = tile
        return 0

    for half in range(2):
        sent = sbuf.at[half, pl.ds(1, N - 1)]
        pltpu.make_async_copy(sent, sent, sem_r.at[half]).wait()
        lax.fori_loop(0, N, functools.partial(widen, half), 0, unroll=16)
        lax.fori_loop(0, 8, coadd, 0, unroll=8)
        lax.fori_loop(0, 16, functools.partial(lay, half), 0, unroll=16)
        for copy in rims[3 * half : 3 + 5 * half]:
            copy.start()

    for half in range(2):
        sent = sbuf.at[half, pl.ds(1, N - 1)]
        pltpu.make_async_copy(sent, sent, sem_s.at[half]).wait()
    everywhere = pl.ds(0, PCOLS + 256)
    parts = ((centre, across), (above, everywhere), (below, everywhere), (centre, left), (centre, right))
    for n, where in enumerate(parts):
        outs.append(pltpu.make_async_copy(fr.at[where], fr_h.at[where], sem_out.at[2 + n]))
    outs[2].start()
    for copy in rims:
        copy.wait()
    for copy in outs[3:]:
        copy.start()
    for copy in outs:
        copy.wait()


def filter_kernel(fr_h, frow_h, fcol_h, coadded, matched, fr, frow_m, fcol_m, sb, out, sem):
    c = lax.axis_index("ccd")
    ins = [pltpu.make_async_copy(frow_h, frow_m, sem.at[0]), pltpu.make_async_copy(fcol_h, fcol_m, sem.at[1])]
    for n in range(3):
        cols = pl.ds(n * 768, 768)
        ins.append(pltpu.make_async_copy(fr_h.at[:, cols], fr.at[:, cols], sem.at[2 + n]))
    for copy in ins:
        copy.start()
    outs = []
    ins[0].wait()
    ins[1].wait()

    done = 0
    for n in range(3):
        ins[2 + n].wait()
        left, right = max(768 * n, 128), min(768 * n + 768, 128 + PCOLS)
        centre = fr.at[pl.ds(RIM, PROWS), pl.ds(left, right - left)]
        outs.append(pltpu.make_async_copy(centre, coadded.at[:, pl.ds(left - 128, right - left)], sem.at[5 + n]))
        outs[-1].start()
        for i in range(3 * n, 3 * n + 3):
            got = dot(frow_m[...], fr[:, pl.ds(i * 256, 256)]).astype(BF16)
            for half in range(2):
                tile = got[:, 128 * half : 128 * half + 128]
                if i == 0 and half == 0:
                    tile = jnp.where(c == 0, jnp.zeros_like(tile), tile)
                if i == 8 and half == 1:
                    tile = jnp.where(c == 31, jnp.zeros_like(tile), tile)
                sb[pl.ds(i * 256 + half * 128, 128), :] = tile
        ready = 6 * n + 4
        for j in range(done, ready):
            three = jnp.concatenate([sb[pl.ds((j + p) * 128, 128), :] for p in range(3)], axis=1)
            out[:, pl.ds(j * 128, 128)] = dot(three, fcol_m[...])
        cols = pl.ds(done * 128, (ready - done) * 128)
        outs.append(pltpu.make_async_copy(out.at[:, cols], matched.at[:, cols], sem.at[8 + n]))
        outs[-1].start()
        done = ready
    for copy in outs:
        copy.wait()


def on_device(exposure, offsets, fraction, route_patch, route_slot, block_weight, kernel_rows, kernel_columns):
    hbm = pl.BlockSpec(memory_space=pltpu.HBM)
    dma = pltpu.SemaphoreType.DMA
    framed = pl.pallas_call(
        kernel,
        out_shape=(
            jax.ShapeDtypeStruct((PROWS + 2 * RIM, PCOLS + 256), BF16),
            jax.ShapeDtypeStruct((PROWS, PROWS + 2 * RIM), BF16),
            jax.ShapeDtypeStruct((384, 128), BF16),
        ),
        in_specs=[hbm] * 8,
        out_specs=(hbm,) * 3,
        scratch_shapes=[
            pltpu.VMEM((EXT, COLS), BF16),
            pltpu.VMEM((TILES + 2, 64, 128), BF16),
            pltpu.VMEM((2, TILES * 2, 16, 128), BF16),
            pltpu.VMEM((2, N, 32, 128), BF16),
            pltpu.VMEM((2, N, 32, 128), BF16),
            pltpu.VMEM((N * 40, 128), F32),
            pltpu.VMEM((16 * 72, 128), F32),
            pltpu.VMEM((PROWS + 2 * RIM, PCOLS + 256), BF16),
            pltpu.VMEM((ROWS, EXT), BF16),
            pltpu.VMEM((384, 128), BF16),
            pltpu.VMEM((PROWS, PROWS + 2 * RIM), BF16),
            pltpu.VMEM((384, 128), BF16),
            pltpu.VMEM((64, 256), BF16),
            pltpu.VMEM((N, 1, 128), F32),
            pltpu.SMEM((1, 1, 2), I32),
            pltpu.SMEM((1, 1, 2), F32),
            pltpu.VMEM((1, 64), I32),
            pltpu.VMEM((1, 64), I32),
            pltpu.VMEM((1, 64), BF16),
            pltpu.SMEM((TAPS,), F32),
            pltpu.SMEM((TAPS,), F32),
            pltpu.VMEM((2, 128), I32),
            pltpu.SMEM((2, 128), I32),
            dma,
            dma((8,)),
            dma((4, PARTS)),
            pltpu.SemaphoreType.REGULAR,
            dma((2,)),
            dma((2,)),
            dma((2,)),
            dma((2, 8)),
            dma((7,)),
        ],
        compiler_params=pltpu.CompilerParams(
            collective_id=0, has_side_effects=True, vmem_limit_bytes=60 * 2**20
        ),
    )(exposure, offsets, fraction, route_patch, route_slot, block_weight, kernel_rows, kernel_columns)
    return pl.pallas_call(
        filter_kernel,
        out_shape=(
            jax.ShapeDtypeStruct((PROWS, PCOLS), BF16),
            jax.ShapeDtypeStruct((PROWS, PCOLS), F32),
        ),
        in_specs=[hbm] * 3,
        out_specs=(hbm, hbm),
        scratch_shapes=[
            pltpu.VMEM((PROWS + 2 * RIM, PCOLS + 256), BF16),
            pltpu.VMEM((PROWS, PROWS + 2 * RIM), BF16),
            pltpu.VMEM((384, 128), BF16),
            pltpu.VMEM((18 * 128, 128), BF16),
            pltpu.VMEM((PROWS, PCOLS), F32),
            dma((11,)),
        ],
        compiler_params=pltpu.CompilerParams(vmem_limit_bytes=60 * 2**20),
    )(*framed)


def solution(mesh):
    placed = (
        P("visit", "ccd", None),
        P("visit", "ccd", None),
        P("visit", "ccd", None),
        P("visit", "ccd"),
        P("visit", "ccd"),
        P("visit", "ccd"),
        P(),
        P(),
    )
    return jax.shard_map(
        on_device,
        mesh=mesh,
        in_specs=placed,
        out_specs=(P("visit", "ccd"), P("visit", "ccd")),
        check_vma=False,
    )
```
